128 devices in a mesh: section: 2 (over x_hi), dp: 16 (over x_lo, y, core), mp: 4 (over z).
Axes of the slice: x: 4 (x_hi: 2, x_lo: 2; x = x_hi * 2 + x_lo), y: 4, z: 4, core: 2. Of those that a mesh axis runs over, the one named last changes fastest.
Arguments:
- hidden: bfloat16 [32, 256, 8192], P(('section', 'dp'), None, 'mp'), may hold values from -6 to 6
- query_weight: bfloat16 [2, 8192, 4096], P('section', None, 'mp'), may hold values from -1 to 1
- keyval_weight: bfloat16 [2, 8192, 2, 512], P('section', None, None, 'mp'), may hold values from -1 to 1
- reward_head: float32 [4096], P('mp'), may hold values from -6 to 6
- lengths: int32 [32], replicated, may hold values from 1 to 256, as said below
- group_ids: int32 [32], replicated, may hold values from 0 to 7, as said below
- dest: int32 [1024, 1], P(('section', 'dp')), may hold values from 0 to 31; in each aligned block of 32 rows (0 to 31, 32 to 63, ...) at most 2 rows name the same one
Outputs:
- relayed: bfloat16 [32, 32, 2, 16, 4096], P(('section', 'dp'), None, None, None, 'mp')
- advantage: float32 [32], P(('section', 'dp'))
The draws below stay inside these ranges and needn't reach their ends.
Inputs may be any that keep to these rules, and one draw needn't show every extreme that they name: `lengths`: at least one row has length 256. `group_ids`: each group id names exactly 4 rows. `dest`: among the 32 blocks of one source no shard is named more than 2 times.
All inputs are finite; a program needn't handle non-finite values.
Results may differ from the reference program's by a relative error of at most 0.0065.
Values may be sent and summed in bfloat16 or wider, within the bound.
No kernel may reach another device: no remote copies, remote signals or barrier semaphores. Data moves between devices by JAX's collectives and lax.ppermute only.
A program may use at most 128 MiB of HBM per device.

```python
import math
import jax
import jax.numpy as jnp
import numpy as np
from jax import lax

D = 8192
HEADS = 32
KVH = 4
HD = 128
L = 256
BLK = 16
GSIZE = 4
ROWS = 32
NBLK = 32
MOST = 2
N_SECTION = 2
N_DP = 16


def draw_lengths(key, part):
    key = jax.random.fold_in(key, 11)
    first_key, second_key = jax.random.split(key)
    offset = jax.random.randint(first_key, (ROWS,), 0, L - L // 8 + 1)
    longest = jax.random.randint(second_key, (), 0, ROWS)
    offset = jnp.where(jnp.arange(ROWS) == longest, 0, offset)
    return (L - offset).astype(jnp.int32)


def draw_group_ids(key, part):
    key = jax.random.fold_in(key, 23)
    return (jax.random.permutation(key, ROWS) // GSIZE).astype(jnp.int32)


def draw_query_weight(key, part):
    noise_key = jax.random.fold_in(key, 31)
    values = jax.random.normal(noise_key, (N_SECTION, D, HEADS * HD), jnp.float32)
    return jnp.clip(values * D ** (-0.5), -1.0, 1.0).astype(jnp.bfloat16)


def draw_keyval_weight(key, part):
    noise_key = jax.random.fold_in(key, 37)
    values = jax.random.normal(noise_key, (N_SECTION, D, 2, KVH * HD), jnp.float32)
    return jnp.clip(values * D ** (-0.5), -1.0, 1.0).astype(jnp.bfloat16)


def level_of(key, extent, cuts, least, largest):
    factor_of = 1.0
    for dim, shards_of in cuts:
        heights = jax.random.uniform(jax.random.fold_in(jax.random.fold_in(key, 6), dim), (shards_of,), jnp.float32, least / len(cuts), largest / len(cuts))
        factor_of = factor_of * jnp.repeat(jnp.exp(heights), extent[dim] // shards_of).reshape((-1,) + (1,) * (len(extent) - 1 - dim))
    return factor_of


def deal_out(key, own, number, rows, count, top, bound, slope):
    order = jax.random.permutation(key, count)
    crowded, common = portions_of(count, rows * top, bound, slope, True), portions_of(count, rows * top, bound, slope, False)
    places = jnp.arange(count)

    def named(sizes, rotation):
        used = int((sizes > 0).sum())
        fixed = max(1, used // 4)
        shifted = fixed + (places - fixed + rotation * (used - fixed)) % max(1, count - fixed)
        return jnp.zeros((count,), jnp.int32).at[order[jnp.where(places < fixed, places, shifted)]].set(jnp.asarray(sizes, jnp.int32))

    sizes = jnp.where(number % 4 == 0, named(crowded, number // 4), named(common, number - number // 4 - 1))
    mixed = jax.random.permutation(jax.random.fold_in(own, 3), count)
    giver, sink = mixed[0:count // 2 * 2:2], mixed[1:count // 2 * 2:2]
    slack = jnp.minimum(sizes[giver] - 1, bound - sizes[sink]) // 2
    slack = jnp.where((giver == order[0]) | (sink == order[0]) | (sizes[sink] == 0), 0, jnp.maximum(slack, 0))
    shifted = jax.random.randint(jax.random.fold_in(own, 4), (count // 2,), 0, 1 << 20) % (slack + 1)
    sizes = sizes.at[giver].add(-shifted).at[sink].add(shifted)
    items = jnp.searchsorted(jnp.cumsum(sizes), jnp.arange(rows * top), side="right").astype(jnp.int32)
    table = items.reshape(top, rows).T
    table = table[jax.random.permutation(jax.random.fold_in(own, 1), rows)]
    rotation = jax.random.randint(jax.random.fold_in(own, 2), (rows, 1), 0, top)
    return jnp.take_along_axis(table, (jnp.arange(top)[None, :] + rotation) % top, axis=1)


def portions_of(number_of, total, reach, lean, full):
    portions = [(1 << 20) // math.isqrt(standing ** lean) + 1 for standing in range(1, number_of + 1)]
    largest = reach if full else min(reach, max(-(-total // number_of), total * portions[0] // sum(portions)))
    least = 1 if total - largest >= number_of - 1 else 0
    holding, rest = [largest] + [least] * (number_of - 1), total - largest - least * (number_of - 1)
    while rest > 0:
        candidates = [i for i in range(1, number_of) if holding[i] < largest] or [i for i in range(1, number_of) if holding[i] < reach]
        mass, remaining = sum([portions[i] for i in candidates]), rest
        for i in candidates:
            more = min(reach - holding[i], max(1, remaining * portions[i] // mass), rest)
            holding[i] = holding[i] + more
            rest = rest - more
    return np.array(holding)


def noise(rng, shape, scale, limit, pieces=(), dtype=jnp.bfloat16):
    array = jax.random.normal(rng, shape, jnp.float32) * scale
    if len(pieces) > 0:
        array = level_of(rng, shape, pieces, -0.22, 0.18) * array
    return jnp.clip(array, min=-limit, max=limit).astype(dtype)


def setup_inputs(seed: int = 0) -> dict:
    streams_of = jax.random.split(jax.random.key(seed), 8)
    hidden = noise(streams_of[0], (ROWS, L, D), 1.0, 6.0, ((0, 32), (2, 4)))
    query_weight = draw_query_weight(jax.random.fold_in(streams_of[7], 71), 0)
    keyval_weight = draw_keyval_weight(jax.random.fold_in(streams_of[7], 71), 0)
    reward_head = noise(streams_of[3], (HEADS * HD,), 1.0, 6.0, ((0, 4),), jnp.float32)
    lengths = draw_lengths(jax.random.fold_in(streams_of[7], 71), 0)
    group_ids = draw_group_ids(jax.random.fold_in(streams_of[7], 71), 0)
    dest_keys = jax.random.split(jax.random.fold_in(streams_of[6], 1), (ROWS * NBLK) // NBLK)
    dest_turns = jax.random.permutation(jax.random.fold_in(streams_of[6], 3), (ROWS * NBLK) // NBLK)
    dest = jax.vmap(lambda own, number: deal_out(jax.random.fold_in(streams_of[6], 2), own, number, NBLK, ROWS, 1, MOST, 2))(dest_keys, dest_turns).reshape((ROWS * NBLK, 1))
    return {"hidden": hidden, "query_weight": query_weight, "keyval_weight": keyval_weight, "reward_head": reward_head, "lengths": lengths, "group_ids": group_ids, "dest": dest}


def attend(query, keys, values, length):
    seq = query.shape[0]
    kv_heads = keys.shape[1] // HD
    heads = query.shape[1] // HD
    group = heads // kv_heads
    q_heads = query.reshape(seq, kv_heads, group, HD).astype(jnp.float32)
    k_heads = keys.reshape(seq, kv_heads, HD).astype(jnp.float32)
    v_heads = values.reshape(seq, kv_heads, HD).astype(jnp.float32)
    scores = jnp.einsum('tkgd,skd->kgts', q_heads, k_heads) * (1.0 / math.sqrt(HD))
    places = jnp.arange(seq)
    allowed = (places[None, :] <= places[:, None]) & (places[None, :] < length)
    scores = jnp.where(allowed, scores, -1e+30)
    highest = lax.optimization_barrier(jnp.max(scores, axis=-1, keepdims=True))
    probs = jnp.exp(scores - highest)
    probs = probs / lax.optimization_barrier(jnp.sum(probs, axis=-1, keepdims=True))
    weights = probs.astype(jnp.bfloat16)
    output = jnp.einsum('kgts,skd->tkgd', weights.astype(jnp.float32), v_heads)
    output = jnp.where((places < length)[:, None, None, None], output, 0.0)
    return output.reshape(seq, heads * HD).astype(jnp.bfloat16)

def route_blocks(blocks, targets, shards, most):
    count = targets.shape[0]
    order = jnp.arange(count)
    same = (targets[:, None] == targets[None, :]) & (order[None, :] < order[:, None])
    rank = lax.optimization_barrier(jnp.sum(same.astype(jnp.int32), axis=1))
    slot = targets * most + rank
    onehot = (jnp.arange(shards * most)[:, None] == slot[None, :]).astype(jnp.bfloat16)
    return jnp.dot(onehot, blocks, preferred_element_type=jnp.float32).astype(jnp.bfloat16)

def reference(hidden, query_weight, keyval_weight, reward_head, lengths, group_ids, dest):
    features = HEADS * HD
    per_model = []
    for model in range(N_SECTION):
        wq_model = query_weight[model]
        wkv_model = keyval_weight[model].reshape(D, 2 * KVH * HD)

        def one_row(item):
            row, length = item
            query = jnp.dot(row, wq_model, preferred_element_type=jnp.float32).astype(jnp.bfloat16)
            keyval = jnp.dot(row, wkv_model, preferred_element_type=jnp.float32).astype(jnp.bfloat16)
            keyval = keyval.reshape(L, 2, KVH * HD)
            return attend(query, keyval[:, 0], keyval[:, 1], length)
        per_model.append(lax.map(one_row, (hidden, lengths)))
    reward = lax.optimization_barrier(jnp.sum(per_model[1].astype(jnp.float32) * reward_head[None, None, :], axis=(1, 2)))
    reward = reward / lengths.astype(jnp.float32)
    member = group_ids[:, None] == jnp.arange(ROWS // GSIZE)[None, :]
    means = lax.optimization_barrier(jnp.sum(jnp.where(member, reward[:, None], 0.0), axis=0)) / GSIZE
    advantage = reward - lax.optimization_barrier(jnp.sum(jnp.where(member, means[None, :], 0.0), axis=1))
    sources = []
    for model in range(N_SECTION):
        states = per_model[model].reshape(N_SECTION, N_DP, L, features)
        states = jnp.transpose(states, (1, 0, 2, 3)).reshape(N_DP, NBLK, BLK * features)
        sources.append(states)
    sources = jnp.concatenate(sources, axis=0)
    targets = dest.reshape(ROWS, NBLK)

    def send_one(item):
        blocks, target_row = item
        return route_blocks(blocks, target_row, ROWS, MOST)
    sent = lax.map(send_one, (sources, targets))
    relayed = jnp.transpose(sent.reshape(ROWS, ROWS, MOST, BLK, features), (1, 0, 2, 3, 4))
    return (relayed, advantage)
```

```python
import functools
import math

import jax
import jax.numpy as jnp
from jax import lax
from jax.experimental import pallas as pl
from jax.experimental.pallas import tpu as pltpu
from jax.sharding import PartitionSpec as P

HD = 128
BLK = 16
GSIZE = 4
LANES = 128
DEPTH = 1024
PLANE = ("section", "dp")
VMEM_LIMIT = 48 * 1024 * 1024


def x_opposite(sections, dp_size):
    count = sections * dp_size
    return [(i, (i + dp_size) % count) for i in range(count)]


def ring(size, step):
    return [(i, (i + step) % size) for i in range(size)]


def project(step, depth_steps, pieces, query_weight, keyval_weight, total):
    features = query_weight.shape[-1]
    piece_step = lax.rem(step, depth_steps)
    for number, (low, high) in enumerate(pieces):
        @pl.when(step // depth_steps == number)
        def _():
            columns = pl.ds(pl.multiple_of(piece_step * DEPTH, DEPTH), DEPTH)
            rows = jnp.concatenate([low[:, columns], high[:, columns]], axis=0)
            total[:, :features] += jnp.dot(rows, query_weight[0], preferred_element_type=jnp.float32)
            total[:, features:] += jnp.dot(rows, keyval_weight[...], preferred_element_type=jnp.float32)


def first_kernel(depth_steps, places, *refs):
    pieces, (query_weight, keyval_weight, total) = refs[:-3], refs[-3:]
    step = pl.program_id(0)

    @pl.when(step == 0)
    def _():
        total[...] = jnp.zeros_like(total)

    project(step, depth_steps, list(zip(pieces[0::2], pieces[1::2])), query_weight, keyval_weight, total)


def attend(total, features, length, states, base):
    seq = total.shape[0]
    half = seq // 2
    keys = total[:, features:features + HD].astype(jnp.bfloat16)
    values = total[:, features + HD:features + 2 * HD].astype(jnp.bfloat16)
    values = jnp.concatenate([values, jnp.ones_like(values)], axis=1)
    scale = math.log2(math.e) / math.sqrt(HD)
    for head in range(features // HD):
        cols = pl.ds(head * HD, HD)
        for begin, size in ((0, half), (half, half)):
            reach = begin + size
            query = total[begin:reach, cols].astype(jnp.bfloat16)
            scores = lax.dot_general(
                query, keys[:reach], (((1,), (1,)), ((), ())), preferred_element_type=jnp.float32
            )
            token = lax.broadcasted_iota(jnp.int32, scores.shape, 0) + begin
            place = lax.broadcasted_iota(jnp.int32, scores.shape, 1)
            scores = jnp.where(place <= token, scores, -1e30)
            highest = jnp.max(scores, axis=1, keepdims=True)
            weights = jnp.exp2((scores - highest) * scale).astype(jnp.bfloat16)
            mixed = jnp.dot(weights, values[:reach], preferred_element_type=jnp.float32)
            output = mixed[:, :HD] / mixed[:, HD:]
            token = lax.broadcasted_iota(jnp.int32, output.shape, 0) + begin
            output = jnp.where(token < length, output, 0.0)
            states[pl.ds(base + begin, size), cols] = output.astype(jnp.bfloat16)


def row_reward(states, base, seq, head, scale, place):
    terms = states[pl.ds(base, seq), :].astype(jnp.float32) * head[...]
    summed = jnp.sum(jnp.sum(terms, axis=0, keepdims=True), axis=1, keepdims=True) * scale
    lane = lax.broadcasted_iota(jnp.int32, (1, LANES), 1)
    return jnp.where(lane == place, jnp.broadcast_to(summed, (1, LANES)), 0.0)


def row_kernel(depth_steps, places, low, high, query_weight, keyval_weight, partial, head, scale, states, reward, total):
    step = pl.program_id(0)

    @pl.when(step == 0)
    def _():
        total[...] = partial[...]

    project(step, depth_steps, [(low, high)], query_weight, keyval_weight, total)

    @pl.when(step == pl.num_programs(0) - 1)
    def _():
        seq = total.shape[0]
        attend(total, query_weight.shape[-1], places[1], states, 0)
        reward[...] = row_reward(states, 0, seq, head, scale[...], places[2])


def last_kernel(
    depth_steps, places, low, high, query_weight, keyval_weight, partial, head, scale, first_states, first_reward,
    outgoing, reward, total, states,
):
    step = pl.program_id(0)
    seq = total.shape[0]

    @pl.when(step == 0)
    def _():
        total[...] = partial[...]
        states[pl.ds(0, seq), :] = first_states[...]

    project(step, depth_steps, [(low, high)], query_weight, keyval_weight, total)

    @pl.when(step == pl.num_programs(0) - 1)
    def _():
        attend(total, query_weight.shape[-1], places[1], states, seq)
        reward[...] = first_reward[...] + row_reward(states, seq, seq, head, scale[...], places[2])
        shards, most = outgoing.shape[0], outgoing.shape[1]

        def fill(shard, carry):
            for k in range(most):
                block = places[3 + shard * most + k]

                @pl.when(block >= 0)
                def _():
                    outgoing[shard, k] = states[pl.ds(pl.multiple_of(block * BLK, BLK), BLK), :]

                @pl.when(block < 0)
                def _():
                    outgoing[shard, k] = jnp.zeros(outgoing.shape[2:], outgoing.dtype)
            return carry

        lax.fori_loop(0, shards, fill, 0)


def whole(shape):
    return pl.BlockSpec(shape, lambda i, places: (0,) * len(shape))


def weight_specs(depth_steps, features):
    def place(i, places):
        return places[i // depth_steps] * depth_steps + i % depth_steps

    return [
        pl.BlockSpec((1, DEPTH, features), lambda i, places: (0, place(i, places), 0)),
        pl.BlockSpec((DEPTH, 2 * HD), lambda i, places: (place(i, places), 0)),
    ]


def estimate(seq, depth, width):
    return pl.CostEstimate(flops=2 * seq * depth * width, bytes_accessed=2 * depth * width, transcendentals=0)


def body(hidden, query_weight, keyval_weight, reward_head, lengths, group_ids, dest):
    sections = lax.axis_size("section")
    dp_size = lax.axis_size("dp")
    mp_size = lax.axis_size("mp")
    section_idx = lax.axis_index("section")
    dp_idx = lax.axis_index("dp")
    mp_idx = lax.axis_index("mp")
    total_rows = lengths.shape[0]
    own = section_idx * dp_size + dp_idx
    other = (1 - section_idx) * dp_size + dp_idx

    seq, depth = hidden.shape[1], hidden.shape[2]
    features = query_weight.shape[2]
    width = features + 2 * HD
    half = seq // 2
    depth_steps = depth // DEPTH
    keyval_weight = keyval_weight.reshape(keyval_weight.shape[1], 2 * HD)

    up = functools.partial(lax.ppermute, axis_name="mp", perm=ring(mp_size, 1))
    down = functools.partial(lax.ppermute, axis_name="mp", perm=ring(mp_size, -1))
    across = functools.partial(lax.ppermute, axis_name=PLANE, perm=x_opposite(sections, dp_size))

    mine_low, mine_high = hidden[0, :half], hidden[0, half:]
    below_low = up(mine_low)
    above_high = down(mine_high)
    theirs = across(hidden[0])
    below_high = up(mine_high)
    above_low = down(mine_low)
    far_low = up(below_low)
    far_high = down(above_high)
    theirs_low, theirs_high = theirs[:half], theirs[half:]
    their_below_low = across(below_low)
    their_above_high = across(above_high)
    their_below_high = up(theirs_high)
    their_above_low = down(theirs_low)
    their_far_low = up(their_below_low)
    their_far_high = down(their_above_high)

    block_count = dest.shape[0]
    most = max(2, 2 * block_count // total_rows)
    targets = dest[:, 0]
    order = jnp.arange(block_count, dtype=jnp.int32)
    same = (targets[:, None] == targets[None, :]) & (order[None, :] < order[:, None])
    slot = targets * most + jnp.sum(same.astype(jnp.int32), axis=1)
    held = jnp.where(section_idx == 0, order, (order + block_count // 2) % block_count)
    hit = jnp.arange(total_rows * most, dtype=jnp.int32)[:, None] == slot[None, :]
    source = jnp.sum(jnp.where(hit, held[None, :] + 1, 0), axis=1) - 1

    below, above, far = (mp_idx + mp_size - 1) % mp_size, (mp_idx + 1) % mp_size, (mp_idx + 2) % mp_size
    three = jnp.stack([mp_idx, below, above]).astype(jnp.int32)
    head = reward_head.reshape(1, features)
    reward_scale = jnp.where(section_idx == 1, 1.0 / lengths.astype(jnp.float32), 0.0)

    def first(pieces):
        return pl.pallas_call(
            functools.partial(first_kernel, depth_steps),
            grid_spec=pltpu.PrefetchScalarGridSpec(
                num_scalar_prefetch=1,
                grid=(depth_steps * len(pieces) // 2,),
                in_specs=[whole((half, depth))] * len(pieces) + weight_specs(depth_steps, features),
                out_specs=whole((seq, width)),
            ),
            out_shape=jax.ShapeDtypeStruct((seq, width), jnp.float32),
            compiler_params=pltpu.CompilerParams(vmem_limit_bytes=VMEM_LIMIT),
            cost_estimate=estimate(seq, depth * len(pieces) // 2, width),
        )(three, *pieces, query_weight, keyval_weight)

    def row_places(row, *more):
        return jnp.concatenate([jnp.stack([far, lengths[row], row]).astype(jnp.int32), *more])

    row_specs = [whole((half, depth))] * 2 + weight_specs(depth_steps, features)
    row_specs += [whole((seq, width)), whole((1, features)), whole((1, 1))]

    own_partial = first([mine_low, mine_high, below_low, below_high, above_low, above_high])
    own_states, own_reward = pl.pallas_call(
        functools.partial(row_kernel, depth_steps),
        grid_spec=pltpu.PrefetchScalarGridSpec(
            num_scalar_prefetch=1,
            grid=(depth_steps,),
            in_specs=row_specs,
            out_specs=[whole((seq, features)), whole((1, LANES))],
            scratch_shapes=[pltpu.VMEM((seq, width), jnp.float32)],
        ),
        out_shape=[
            jax.ShapeDtypeStruct((seq, features), jnp.bfloat16),
            jax.ShapeDtypeStruct((1, LANES), jnp.float32),
        ],
        compiler_params=pltpu.CompilerParams(vmem_limit_bytes=VMEM_LIMIT),
        cost_estimate=estimate(seq, depth, width),
    )(row_places(own), far_low, far_high, query_weight, keyval_weight, own_partial, head, reward_scale[own].reshape(1, 1))

    their_partial = first([theirs_low, theirs_high, their_below_low, their_below_high, their_above_low, their_above_high])
    outgoing, rewards = pl.pallas_call(
        functools.partial(last_kernel, depth_steps),
        grid_spec=pltpu.PrefetchScalarGridSpec(
            num_scalar_prefetch=1,
            grid=(depth_steps,),
            in_specs=row_specs + [whole((seq, features)), whole((1, LANES))],
            out_specs=[whole((total_rows, most, BLK, features)), whole((1, LANES))],
            scratch_shapes=[pltpu.VMEM((seq, width), jnp.float32), pltpu.VMEM((2 * seq, features), jnp.bfloat16)],
        ),
        out_shape=[
            jax.ShapeDtypeStruct((total_rows, most, BLK, features), jnp.bfloat16),
            jax.ShapeDtypeStruct((1, LANES), jnp.float32),
        ],
        compiler_params=pltpu.CompilerParams(vmem_limit_bytes=VMEM_LIMIT),
        cost_estimate=estimate(seq, depth, width),
    )(
        row_places(other, source), their_far_low, their_far_high, query_weight, keyval_weight, their_partial, head,
        reward_scale[other].reshape(1, 1), own_states, own_reward,
    )

    received = lax.all_to_all(outgoing, PLANE, split_axis=0, concat_axis=0, tiled=True)

    for step in (1, 2):
        rewards += lax.ppermute(rewards, "mp", [(i, i ^ step) for i in range(mp_size)])
    step = 1
    while step < sections * dp_size:
        rewards += lax.ppermute(rewards, PLANE, [(i, i ^ step) for i in range(sections * dp_size)])
        step *= 2
    rewards = rewards[0, :total_rows]
    alike = group_ids == group_ids[own]
    advantage = rewards[own] - jnp.sum(jnp.where(alike, rewards, 0.0)) / GSIZE
    return (received[None], advantage[None])


def solution(mesh):
    return jax.shard_map(
        body,
        mesh=mesh,
        in_specs=(
            P(("section", "dp"), None, "mp"),
            P("section", None, "mp"),
            P("section", None, None, "mp"),
            P("mp"),
            P(),
            P(),
            P(("section", "dp"), None),
        ),
        out_specs=(P(("section", "dp"), None, None, None, "mp"), P(("section", "dp"))),
        check_vma=False,
    )
```

```python
import functools
import math

import jax
import jax.numpy as jnp
from jax import lax
from jax.experimental import pallas as pl
from jax.experimental.pallas import tpu as pltpu
from jax.sharding import PartitionSpec as P

HD = 128
BLK = 16
GSIZE = 4
LANES = 128
START_TILE = 1024
MIDDLE_TILE = 2048
LAST_TILE = 1024
END = 80
PASSED = 80
PLANE = ("section", "dp")
VMEM_LIMIT = 32 * 1024 * 1024


def x_opposite(sections, dp_size):
    count = sections * dp_size
    return [(i, (i + dp_size) % count) for i in range(count)]


def ring(size, step):
    return [(i, (i + step) % size) for i in range(size)]


def turn(count, span, size, step):
    return [(i, i + ((i // span + step) % size - i // span % size) * span) for i in range(count)]


def project(parts, query_weight, keyval_weight, total):
    features = query_weight.shape[-1]
    rows = jnp.concatenate(parts, axis=0)
    total[:, :features] += jnp.dot(rows, query_weight[0], preferred_element_type=jnp.float32)
    total[:, features:] += jnp.dot(rows, keyval_weight[...], preferred_element_type=jnp.float32)


def project_kernel(depth_steps, number, places, *refs):
    parts, (partial, query_weight, keyval_weight, total) = refs[:-4], refs[-4:]
    step = pl.program_id(0)

    @pl.when(step == 0)
    def _():
        total[...] = jnp.zeros_like(total) if partial is None else partial[...]

    each = len(parts) // number
    depth = query_weight.shape[1]
    columns = pl.ds(pl.multiple_of(lax.rem(step, depth_steps) * depth, depth), depth)
    for piece in range(number):
        @pl.when(step // depth_steps == piece)
        def _():
            held = [part[:, columns] for part in parts[piece * each:(piece + 1) * each]]
            project(held, query_weight, keyval_weight, total)


def start_kernel(depth_steps, places, *refs):
    project_kernel(depth_steps, 1, places, *refs[:-3], None, *refs[-3:])


def attend(total, features, length, states, base):
    seq = total.shape[0]
    half = seq // 2
    keys = total[:, features:features + HD].astype(jnp.bfloat16)
    values = total[:, features + HD:features + 2 * HD].astype(jnp.bfloat16)
    values = jnp.concatenate([values, jnp.ones_like(values)], axis=1)
    scale = math.log2(math.e) / math.sqrt(HD)
    for head in range(features // HD):
        cols = pl.ds(head * HD, HD)
        for begin, size in ((0, half), (half, half)):
            reach = begin + size
            query = total[begin:reach, cols].astype(jnp.bfloat16)
            scores = lax.dot_general(
                query, keys[:reach], (((1,), (1,)), ((), ())), preferred_element_type=jnp.float32
            )
            token = lax.broadcasted_iota(jnp.int32, scores.shape, 0) + begin
            place = lax.broadcasted_iota(jnp.int32, scores.shape, 1)
            scores = jnp.where(place <= token, scores, -1e30)
            highest = jnp.max(scores, axis=1, keepdims=True)
            weights = jnp.exp2((scores - highest) * scale).astype(jnp.bfloat16)
            mixed = jnp.dot(weights, values[:reach], preferred_element_type=jnp.float32)
            output = mixed[:, :HD] / mixed[:, HD:]
            token = lax.broadcasted_iota(jnp.int32, output.shape, 0) + begin
            output = jnp.where(token < length, output, 0.0)
            states[pl.ds(base + begin, size), cols] = output.astype(jnp.bfloat16)


def row_reward(states, base, seq, head, scale, place):
    terms = states[pl.ds(base, seq), :].astype(jnp.float32) * head[...]
    summed = jnp.sum(jnp.sum(terms, axis=0, keepdims=True), axis=1, keepdims=True) * scale
    lane = lax.broadcasted_iota(jnp.int32, (1, LANES), 1)
    return jnp.where(lane == place, jnp.broadcast_to(summed, (1, LANES)), 0.0)


def row_kernel(depth_steps, places, *refs):
    parts, (head, scale, earlier, states, reward, total) = refs[:-6], refs[-6:]
    project_kernel(depth_steps, 1, places, *parts, total)

    @pl.when(pl.program_id(0) == pl.num_programs(0) - 1)
    def _():
        attend(total, states.shape[1], places[1], states, 0)
        reward[...] = earlier[...] + row_reward(states, 0, total.shape[0], head, scale[...], places[2])


def place_kernel(slots, first, second, outgoing):
    shards, most = outgoing.shape[0], outgoing.shape[1]
    seq = first.shape[0]

    def fill(shard, carry):
        for k in range(most):
            block = slots[shard * most + k]
            rows = pl.ds(pl.multiple_of(lax.rem(jnp.maximum(block, 0), seq // BLK) * BLK, BLK), BLK)
            held = jnp.where(block < seq // BLK, first[rows, :], second[rows, :])
            outgoing[shard, k] = jnp.where(block >= 0, held, jnp.zeros_like(held))
        return carry

    lax.fori_loop(0, shards, fill, 0, unroll=4)


def advantage_kernel(rewards, shares, advantage):
    advantage[...] = jnp.sum(rewards[...] * shares[...], axis=1, keepdims=True)


def whole(shape):
    return pl.BlockSpec(shape, lambda i, places: (0,) * len(shape))


def weight_specs(tile, depth_steps, features):
    def place(i, places):
        return places[i // depth_steps] * depth_steps + i % depth_steps

    return [
        pl.BlockSpec((1, tile, features), lambda i, places: (0, place(i, places), 0)),
        pl.BlockSpec((tile, 2 * HD), lambda i, places: (place(i, places), 0)),
    ]


def estimate(seq, depth, width):
    return pl.CostEstimate(flops=2 * seq * depth * width, bytes_accessed=2 * depth * width, transcendentals=0)


def body(hidden, query_weight, keyval_weight, reward_head, lengths, group_ids, dest):
    sections = lax.axis_size("section")
    dp_size = lax.axis_size("dp")
    mp_size = lax.axis_size("mp")
    section_idx = lax.axis_index("section")
    dp_idx = lax.axis_index("dp")
    mp_idx = lax.axis_index("mp")
    total_rows = lengths.shape[0]
    own = section_idx * dp_size + dp_idx
    other = (1 - section_idx) * dp_size + dp_idx

    seq, depth = hidden.shape[1], hidden.shape[2]
    features = query_weight.shape[2]
    width = features + 2 * HD
    half = seq // 2
    keyval_weight = keyval_weight.reshape(keyval_weight.shape[1], 2 * HD)

    up = functools.partial(lax.ppermute, axis_name="mp", perm=ring(mp_size, 1))
    down = functools.partial(lax.ppermute, axis_name="mp", perm=ring(mp_size, -1))
    across = functools.partial(lax.ppermute, axis_name=PLANE, perm=x_opposite(sections, dp_size))

    block_count = dest.shape[0]
    most = max(2, 2 * block_count // total_rows)
    targets = dest[:, 0]
    order = jnp.arange(block_count, dtype=jnp.int32)
    same = (targets[:, None] == targets[None, :]) & (order[None, :] < order[:, None])
    slot = targets * most + jnp.sum(same.astype(jnp.int32), axis=1)
    held = jnp.where(section_idx == 0, order, (order + block_count // 2) % block_count)
    hit = jnp.arange(total_rows * most, dtype=jnp.int32)[:, None] == slot[None, :]
    source = jnp.sum(jnp.where(hit, held[None, :] + 1, 0), axis=1) - 1

    mine = hidden[0]
    below, above = up(mine), down(mine)
    theirs = across(mine)

    below_idx, above_idx, far_idx = (mp_idx + mp_size - 1) % mp_size, (mp_idx + 1) % mp_size, (mp_idx + 2) % mp_size
    head = reward_head.reshape(1, features)
    reward_scale = jnp.where(section_idx == 1, 1.0 / lengths.astype(jnp.float32), 0.0)

    rows = jnp.arange(total_rows)
    shares = jnp.where(rows == own, 1.0, 0.0) - jnp.where(group_ids == group_ids[own], 1.0 / GSIZE, 0.0)
    shares = jnp.pad(shares, (0, LANES - total_rows)).reshape(1, LANES)

    def indices(*values):
        return jnp.stack([jnp.asarray(value, jnp.int32) for value in values])

    def call(kernel, tile, pieces, places, operands, in_specs, out_specs, out_shape, scratch=()):
        depth_steps = depth // tile
        return pl.pallas_call(
            functools.partial(kernel, depth_steps),
            grid_spec=pltpu.PrefetchScalarGridSpec(
                num_scalar_prefetch=1,
                grid=(depth_steps * pieces,),
                in_specs=in_specs[:-1] + weight_specs(tile, depth_steps, features) + in_specs[-1],
                out_specs=out_specs,
                scratch_shapes=scratch,
            ),
            out_shape=out_shape,
            compiler_params=pltpu.CompilerParams(vmem_limit_bytes=VMEM_LIMIT),
            cost_estimate=estimate(seq, depth * pieces, width),
        )(places, *operands[:-1], query_weight, keyval_weight, *operands[-1])

    total_spec = whole((seq, width))

    def start(piece):
        return call(
            start_kernel, START_TILE, 1, indices(mp_idx), [piece, []], [whole((seq, depth)), []],
            total_spec, jax.ShapeDtypeStruct((seq, width), jnp.float32),
        )

    def middle(parts, total):
        return call(
            lambda steps, *refs: project_kernel(steps, 2, *refs), MIDDLE_TILE, 2, indices(below_idx, above_idx),
            [*parts, total, []], [whole(part.shape) for part in parts] + [total_spec, []],
            total_spec, jax.ShapeDtypeStruct((seq, width), jnp.float32),
        )

    def finish(parts, partial, row, earlier):
        return call(
            row_kernel, LAST_TILE, 1, indices(far_idx, lengths[row], row),
            [*parts, partial, [head, reward_scale[row].reshape(1, 1), earlier]],
            [whole(part.shape) for part in parts]
            + [total_spec, [whole((1, features)), whole((1, 1)), whole((1, LANES))]],
            [whole((seq, features)), whole((1, LANES))],
            [jax.ShapeDtypeStruct((seq, features), jnp.bfloat16), jax.ShapeDtypeStruct((1, LANES), jnp.float32)],
            [pltpu.VMEM((seq, width), jnp.float32)],
        )

    def ahead(*arrays):
        return lax.optimization_barrier(arrays)

    own_start = start(mine)
    below, above, own_start = ahead(below, above, own_start)
    far_low, far_high = up(below[:half]), down(above[half:])
    crossed = across(jnp.concatenate([below[:END], above[seq - END:]], axis=0))
    theirs, below, above = ahead(theirs, below, above)
    own_partial = middle([below, above], own_start)
    theirs, own_partial = ahead(theirs, own_partial)
    their_below_high, their_above_low = up(theirs[END:]), down(theirs[:seq - END])
    theirs, far_low, far_high = ahead(theirs, far_low, far_high)
    far_middle = across(jnp.concatenate([far_low[PASSED:], far_high[:half - PASSED]], axis=0))
    own_states, own_reward = finish([far_low, far_high], own_partial, own, jnp.zeros((1, LANES), jnp.float32))
    their_start = start(theirs)
    crossed, own_states = ahead(crossed, own_states)
    their_far_low, their_far_high = up(crossed[:PASSED]), down(crossed[2 * END - PASSED:])
    their_partial = middle([crossed[:END], their_below_high, their_above_low, crossed[END:]], their_start)
    their_states, rewards = finish([their_far_low, far_middle, their_far_high], their_partial, other, own_reward)

    block_spec = pl.BlockSpec((seq, features), lambda i, slots: (0, 0))
    outgoing = pl.pallas_call(
        place_kernel,
        grid_spec=pltpu.PrefetchScalarGridSpec(
            num_scalar_prefetch=1,
            grid=(1,),
            in_specs=[block_spec, block_spec],
            out_specs=pl.BlockSpec((total_rows, most, BLK, features), lambda i, slots: (0, 0, 0, 0)),
        ),
        out_shape=jax.ShapeDtypeStruct((total_rows, most, BLK, features), jnp.bfloat16),
        compiler_params=pltpu.CompilerParams(vmem_limit_bytes=VMEM_LIMIT),
        cost_estimate=pl.CostEstimate(flops=0, bytes_accessed=6 * seq * features, transcendentals=0),
    )(source, own_states, their_states)
    received = lax.all_to_all(outgoing, PLANE, split_axis=0, concat_axis=0, tiled=True)

    rewards += sum(lax.ppermute(rewards, "mp", ring(mp_size, step)) for step in range(1, mp_size))
    cores = 2
    across_size = sections * 2
    along = sections * dp_size // (cores * across_size)
    for span, size in ((1, cores), (cores, along), (cores * along, across_size)):
        rewards += sum(lax.ppermute(rewards, PLANE, turn(sections * dp_size, span, size, step)) for step in range(1, size))
    advantage = pl.pallas_call(
        advantage_kernel, out_shape=jax.ShapeDtypeStruct((1, 1), jnp.float32)
    )(rewards, shares)
    return (received[None], advantage.reshape(1))


def solution(mesh):
    return jax.shard_map(
        body,
        mesh=mesh,
        in_specs=(
            P(("section", "dp"), None, "mp"),
            P("section", None, "mp"),
            P("section", None, None, "mp"),
            P("mp"),
            P(),
            P(),
            P(("section", "dp"), None),
        ),
        out_specs=(P(("section", "dp"), None, None, None, "mp"), P(("section", "dp"))),
        check_vma=False,
    )
```

```python
import functools
import math

import jax
import jax.numpy as jnp
from jax import lax
from jax.experimental import pallas as pl
from jax.experimental.pallas import tpu as pltpu
from jax.sharding import PartitionSpec as P

HD = 128
BLK = 16
GSIZE = 4
LANES = 128
START_TILE = 1024
MIDDLE_TILE = 2048
LAST_TILE = 1024
END = 80
PASSED = 64
PLANE = ("section", "dp")
VMEM_LIMIT = 32 * 1024 * 1024


def x_opposite(sections, dp_size):
    count = sections * dp_size
    return [(i, (i + dp_size) % count) for i in range(count)]


def ring(size, step):
    return [(i, (i + step) % size) for i in range(size)]


def turn(count, span, size, step):
    return [(i, i + ((i // span + step) % size - i // span % size) * span) for i in range(count)]


def project(parts, query_weight, keyval_weight, total):
    features = query_weight.shape[-1]
    rows = jnp.concatenate(parts, axis=0)
    total[:, :features] += jnp.dot(rows, query_weight[0], preferred_element_type=jnp.float32)
    total[:, features:] += jnp.dot(rows, keyval_weight[...], preferred_element_type=jnp.float32)


def project_kernel(depth_steps, number, places, *refs):
    parts, (partial, query_weight, keyval_weight, total) = refs[:-4], refs[-4:]
    step = pl.program_id(0)

    @pl.when(step == 0)
    def _():
        total[...] = jnp.zeros_like(total) if partial is None else partial[...]

    each = len(parts) // number
    depth = query_weight.shape[1]
    columns = pl.ds(pl.multiple_of(lax.rem(step, depth_steps) * depth, depth), depth)
    for piece in range(number):
        @pl.when(step // depth_steps == piece)
        def _():
            held = [part[:, columns] for part in parts[piece * each:(piece + 1) * each]]
            project(held, query_weight, keyval_weight, total)


def start_kernel(depth_steps, places, *refs):
    project_kernel(depth_steps, 1, places, *refs[:-3], None, *refs[-3:])


def attend(total, features, length, states, base):
    seq = total.shape[0]
    half = seq // 2
    keys = total[:, features:features + HD].astype(jnp.bfloat16)
    values = total[:, features + HD:features + 2 * HD].astype(jnp.bfloat16)
    values = jnp.concatenate([values, jnp.ones_like(values)], axis=1)
    scale = math.log2(math.e) / math.sqrt(HD)
    for head in range(features // HD):
        cols = pl.ds(head * HD, HD)
        for begin, size in ((0, half), (half, half)):
            reach = begin + size
            query = total[begin:reach, cols].astype(jnp.bfloat16)
            scores = lax.dot_general(
                query, keys[:reach], (((1,), (1,)), ((), ())), preferred_element_type=jnp.float32
            )
            token = lax.broadcasted_iota(jnp.int32, scores.shape, 0) + begin
            place = lax.broadcasted_iota(jnp.int32, scores.shape, 1)
            scores = jnp.where(place <= token, scores, -1e30)
            highest = jnp.max(scores, axis=1, keepdims=True)
            weights = jnp.exp2((scores - highest) * scale).astype(jnp.bfloat16)
            mixed = jnp.dot(weights, values[:reach], preferred_element_type=jnp.float32)
            output = mixed[:, :HD] / mixed[:, HD:]
            token = lax.broadcasted_iota(jnp.int32, output.shape, 0) + begin
            output = jnp.where(token < length, output, 0.0)
            states[pl.ds(base + begin, size), cols] = output.astype(jnp.bfloat16)


def row_reward(states, base, seq, head, scale, place):
    terms = states[pl.ds(base, seq), :].astype(jnp.float32) * head[...]
    summed = jnp.sum(jnp.sum(terms, axis=0, keepdims=True), axis=1, keepdims=True) * scale
    lane = lax.broadcasted_iota(jnp.int32, (1, LANES), 1)
    return jnp.where(lane == place, jnp.broadcast_to(summed, (1, LANES)), 0.0)


def row_kernel(depth_steps, places, *refs):
    parts, (head, scale, earlier, states, reward, total) = refs[:-6], refs[-6:]
    project_kernel(depth_steps, 1, places, *parts, total)

    @pl.when(pl.program_id(0) == pl.num_programs(0) - 1)
    def _():
        attend(total, states.shape[1], places[1], states, 0)
        reward[...] = earlier[...] + row_reward(states, 0, total.shape[0], head, scale[...], places[2])


def place_kernel(slots, first, second, outgoing):
    shards, most = outgoing.shape[0], outgoing.shape[1]
    seq = first.shape[0]

    def fill(shard, carry):
        for k in range(most):
            block = slots[shard * most + k]
            rows = pl.ds(pl.multiple_of(lax.rem(jnp.maximum(block, 0), seq // BLK) * BLK, BLK), BLK)
            held = jnp.where(block < seq // BLK, first[rows, :], second[rows, :])
            outgoing[shard, k] = jnp.where(block >= 0, held, jnp.zeros_like(held))
        return carry

    lax.fori_loop(0, shards, fill, 0, unroll=4)


def advantage_kernel(rewards, shares, advantage):
    advantage[...] = jnp.sum(rewards[...] * shares[...], axis=1, keepdims=True)


def whole(shape):
    return pl.BlockSpec(shape, lambda i, places: (0,) * len(shape))


def weight_specs(tile, depth_steps, features):
    def place(i, places):
        return places[i // depth_steps] * depth_steps + i % depth_steps

    return [
        pl.BlockSpec((1, tile, features), lambda i, places: (0, place(i, places), 0)),
        pl.BlockSpec((tile, 2 * HD), lambda i, places: (place(i, places), 0)),
    ]


def estimate(seq, depth, width):
    return pl.CostEstimate(flops=2 * seq * depth * width, bytes_accessed=2 * depth * width, transcendentals=0)


def body(hidden, query_weight, keyval_weight, reward_head, lengths, group_ids, dest):
    sections = lax.axis_size("section")
    dp_size = lax.axis_size("dp")
    mp_size = lax.axis_size("mp")
    section_idx = lax.axis_index("section")
    dp_idx = lax.axis_index("dp")
    mp_idx = lax.axis_index("mp")
    total_rows = lengths.shape[0]
    own = section_idx * dp_size + dp_idx
    other = (1 - section_idx) * dp_size + dp_idx

    seq, depth = hidden.shape[1], hidden.shape[2]
    features = query_weight.shape[2]
    width = features + 2 * HD
    half = seq // 2
    keyval_weight = keyval_weight.reshape(keyval_weight.shape[1], 2 * HD)

    up = functools.partial(lax.ppermute, axis_name="mp", perm=ring(mp_size, 1))
    down = functools.partial(lax.ppermute, axis_name="mp", perm=ring(mp_size, -1))
    across = functools.partial(lax.ppermute, axis_name=PLANE, perm=x_opposite(sections, dp_size))

    block_count = dest.shape[0]
    most = max(2, 2 * block_count // total_rows)
    targets = dest[:, 0]
    order = jnp.arange(block_count, dtype=jnp.int32)
    same = (targets[:, None] == targets[None, :]) & (order[None, :] < order[:, None])
    slot = targets * most + jnp.sum(same.astype(jnp.int32), axis=1)
    held = jnp.where(section_idx == 0, order, (order + block_count // 2) % block_count)
    hit = jnp.arange(total_rows * most, dtype=jnp.int32)[:, None] == slot[None, :]
    source = jnp.sum(jnp.where(hit, held[None, :] + 1, 0), axis=1) - 1

    mine = hidden[0]
    below, above = up(mine), down(mine)
    mine_across, keyval_weight = lax.optimization_barrier((mine, keyval_weight))
    theirs = across(mine_across)

    below_idx, above_idx, far_idx = (mp_idx + mp_size - 1) % mp_size, (mp_idx + 1) % mp_size, (mp_idx + 2) % mp_size
    head = reward_head.reshape(1, features)
    reward_scale = jnp.where(section_idx == 1, 1.0 / lengths.astype(jnp.float32), 0.0)

    rows = jnp.arange(total_rows)
    shares = jnp.where(rows == own, 1.0, 0.0) - jnp.where(group_ids == group_ids[own], 1.0 / GSIZE, 0.0)
    shares = jnp.pad(shares, (0, LANES - total_rows)).reshape(1, LANES)

    def indices(*values):
        return jnp.stack([jnp.asarray(value, jnp.int32) for value in values])

    def call(kernel, tile, pieces, places, operands, in_specs, out_specs, out_shape, scratch=()):
        depth_steps = depth // tile
        return pl.pallas_call(
            functools.partial(kernel, depth_steps),
            grid_spec=pltpu.PrefetchScalarGridSpec(
                num_scalar_prefetch=1,
                grid=(depth_steps * pieces,),
                in_specs=in_specs[:-1] + weight_specs(tile, depth_steps, features) + in_specs[-1],
                out_specs=out_specs,
                scratch_shapes=scratch,
            ),
            out_shape=out_shape,
            compiler_params=pltpu.CompilerParams(vmem_limit_bytes=VMEM_LIMIT),
            cost_estimate=estimate(seq, depth * pieces, width),
        )(places, *operands[:-1], query_weight, keyval_weight, *operands[-1])

    total_spec = whole((seq, width))

    def start(piece):
        return call(
            start_kernel, START_TILE, 1, indices(mp_idx), [piece, []], [whole((seq, depth)), []],
            total_spec, jax.ShapeDtypeStruct((seq, width), jnp.float32),
        )

    def middle(parts, total):
        return call(
            lambda steps, *refs: project_kernel(steps, 2, *refs), MIDDLE_TILE, 2, indices(below_idx, above_idx),
            [*parts, total, []], [whole(part.shape) for part in parts] + [total_spec, []],
            total_spec, jax.ShapeDtypeStruct((seq, width), jnp.float32),
        )

    def finish(parts, partial, row, earlier):
        return call(
            row_kernel, LAST_TILE, 1, indices(far_idx, lengths[row], row),
            [*parts, partial, [head, reward_scale[row].reshape(1, 1), earlier]],
            [whole(part.shape) for part in parts]
            + [total_spec, [whole((1, features)), whole((1, 1)), whole((1, LANES))]],
            [whole((seq, features)), whole((1, LANES))],
            [jax.ShapeDtypeStruct((seq, features), jnp.bfloat16), jax.ShapeDtypeStruct((1, LANES), jnp.float32)],
            [pltpu.VMEM((seq, width), jnp.float32)],
        )

    def ahead(*arrays):
        return lax.optimization_barrier(arrays)

    own_start = start(mine)
    below, above, own_start = ahead(below, above, own_start)
    far_low, far_high = up(below[:half]), down(above[half:])
    crossed = across(jnp.concatenate([below[:END], above[seq - END:]], axis=0))
    own_partial = middle([below, above], own_start)
    theirs, own_partial = ahead(theirs, own_partial)
    their_below_high, their_above_low = up(theirs[END:]), down(theirs[:seq - END])
    theirs, far_low, far_high = ahead(theirs, far_low, far_high)
    far_middle = across(jnp.concatenate([far_low[PASSED:], far_high[:half - PASSED]], axis=0))
    own_states, own_reward = finish([far_low, far_high], own_partial, own, jnp.zeros((1, LANES), jnp.float32))
    their_start = start(theirs)
    crossed, own_states = ahead(crossed, own_states)
    their_far_low, their_far_high = up(crossed[:PASSED]), down(crossed[2 * END - PASSED:])
    their_partial = middle([crossed[:END], their_below_high, their_above_low, crossed[END:]], their_start)
    their_states, rewards = finish([their_far_low, far_middle, their_far_high], their_partial, other, own_reward)

    block_spec = pl.BlockSpec((seq, features), lambda i, slots: (0, 0))
    outgoing = pl.pallas_call(
        place_kernel,
        grid_spec=pltpu.PrefetchScalarGridSpec(
            num_scalar_prefetch=1,
            grid=(1,),
            in_specs=[block_spec, block_spec],
            out_specs=pl.BlockSpec((total_rows, most, BLK, features), lambda i, slots: (0, 0, 0, 0)),
        ),
        out_shape=jax.ShapeDtypeStruct((total_rows, most, BLK, features), jnp.bfloat16),
        compiler_params=pltpu.CompilerParams(vmem_limit_bytes=VMEM_LIMIT),
        cost_estimate=pl.CostEstimate(flops=0, bytes_accessed=6 * seq * features, transcendentals=0),
    )(source, own_states, their_states)
    cores = 2
    across_size = sections * 2
    along = sections * dp_size // (cores * across_size)

    def summed(terms, span, size):
        pairs = [turn(sections * dp_size, span, size, step) for step in range(1, size)]
        return terms + sum(lax.ppermute(terms, PLANE, pair) for pair in pairs)

    rewards = summed(rewards, cores, along)
    outgoing, rewards = ahead(outgoing, rewards)
    received = lax.all_to_all(outgoing, PLANE, split_axis=0, concat_axis=0, tiled=True)
    rewards += sum(lax.ppermute(rewards, "mp", ring(mp_size, step)) for step in range(1, mp_size))
    rewards = summed(rewards, 1, cores)
    rewards = summed(rewards, cores * along, across_size)
    advantage = pl.pallas_call(
        advantage_kernel, out_shape=jax.ShapeDtypeStruct((1, 1), jnp.float32)
    )(rewards, shares)
    return (received[None], advantage.reshape(1))


def solution(mesh):
    return jax.shard_map(
        body,
        mesh=mesh,
        in_specs=(
            P(("section", "dp"), None, "mp"),
            P("section", None, "mp"),
            P("section", None, None, "mp"),
            P("mp"),
            P(),
            P(),
            P(("section", "dp"), None),
        ),
        out_specs=(P(("section", "dp"), None, None, None, "mp"), P(("section", "dp"))),
        check_vma=False,
    )
```

```python
import functools
import math

import jax
import jax.numpy as jnp
from jax import lax
from jax.experimental import pallas as pl
from jax.experimental.pallas import tpu as pltpu
from jax.sharding import PartitionSpec as P

HD = 128
BLK = 16
GSIZE = 4
LANES = 128
START_TILE = 1024
MIDDLE_TILE = 2048
LAST_TILE = 1024
END = 80
PASSED = 64
PLANE = ("section", "dp")
VMEM_LIMIT = 32 * 1024 * 1024


def x_opposite(sections, dp_size):
    count = sections * dp_size
    return [(i, (i + dp_size) % count) for i in range(count)]


def ring(size, step):
    return [(i, (i + step) % size) for i in range(size)]


def turn(count, span, size, step):
    return [(i, i + ((i // span + step) % size - i // span % size) * span) for i in range(count)]


def project(parts, query_weight, keyval_weight, total):
    features = query_weight.shape[-1]
    rows = jnp.concatenate(parts, axis=0)
    total[:, :features] += jnp.dot(rows, query_weight[0], preferred_element_type=jnp.float32)
    total[:, features:] += jnp.dot(rows, keyval_weight[...], preferred_element_type=jnp.float32)


def project_kernel(depth_steps, number, places, *refs):
    parts, (partial, query_weight, keyval_weight, total) = refs[:-4], refs[-4:]
    step = pl.program_id(0)

    @pl.when(step == 0)
    def _():
        total[...] = jnp.zeros_like(total) if partial is None else partial[...]

    each = len(parts) // number
    depth = query_weight.shape[1]
    columns = pl.ds(pl.multiple_of(lax.rem(step, depth_steps) * depth, depth), depth)
    for piece in range(number):
        @pl.when(step // depth_steps == piece)
        def _():
            held = [part[:, columns] for part in parts[piece * each:(piece + 1) * each]]
            project(held, query_weight, keyval_weight, total)


def start_kernel(depth_steps, places, *refs):
    project_kernel(depth_steps, 1, places, *refs[:-3], None, *refs[-3:])


def attend(total, features, length, states, base):
    seq = total.shape[0]
    half = seq // 2
    keys = total[:, features:features + HD].astype(jnp.bfloat16)
    values = total[:, features + HD:features + 2 * HD].astype(jnp.bfloat16)
    values = jnp.concatenate([values, jnp.ones_like(values)], axis=1)
    scale = math.log2(math.e) / math.sqrt(HD)
    for head in range(features // HD):
        cols = pl.ds(head * HD, HD)
        for begin, size in ((0, half), (half, half)):
            reach = begin + size
            query = total[begin:reach, cols].astype(jnp.bfloat16)
            scores = lax.dot_general(
                query, keys[:reach], (((1,), (1,)), ((), ())), preferred_element_type=jnp.float32
            )
            token = lax.broadcasted_iota(jnp.int32, scores.shape, 0) + begin
            place = lax.broadcasted_iota(jnp.int32, scores.shape, 1)
            scores = jnp.where(place <= token, scores, -1e30)
            highest = jnp.max(scores, axis=1, keepdims=True)
            weights = jnp.exp2((scores - highest) * scale).astype(jnp.bfloat16)
            mixed = jnp.dot(weights, values[:reach], preferred_element_type=jnp.float32)
            output = mixed[:, :HD] / mixed[:, HD:]
            token = lax.broadcasted_iota(jnp.int32, output.shape, 0) + begin
            output = jnp.where(token < length, output, 0.0)
            states[pl.ds(base + begin, size), cols] = output.astype(jnp.bfloat16)


def row_reward(states, base, seq, head, scale, place):
    terms = states[pl.ds(base, seq), :].astype(jnp.float32) * head[...]
    summed = jnp.sum(jnp.sum(terms, axis=0, keepdims=True), axis=1, keepdims=True) * scale
    lane = lax.broadcasted_iota(jnp.int32, (1, LANES), 1)
    return jnp.where(lane == place, jnp.broadcast_to(summed, (1, LANES)), 0.0)


def row_kernel(depth_steps, places, *refs):
    parts, (head, scale, earlier, states, reward, total) = refs[:-6], refs[-6:]
    project_kernel(depth_steps, 1, places, *parts, total)

    @pl.when(pl.program_id(0) == pl.num_programs(0) - 1)
    def _():
        attend(total, states.shape[1], places[1], states, 0)
        reward[...] = earlier[...] + row_reward(states, 0, total.shape[0], head, scale[...], places[2])


def place_kernel(slots, first, second, outgoing):
    shards, most = outgoing.shape[0], outgoing.shape[1]
    seq = first.shape[0]

    def fill(shard, carry):
        for k in range(most):
            block = slots[shard * most + k]
            rows = pl.ds(pl.multiple_of(lax.rem(jnp.maximum(block, 0), seq // BLK) * BLK, BLK), BLK)
            held = jnp.where(block < seq // BLK, first[rows, :], second[rows, :])
            outgoing[shard, k] = jnp.where(block >= 0, held, jnp.zeros_like(held))
        return carry

    lax.fori_loop(0, shards, fill, 0, unroll=4)


def advantage_kernel(shares, *refs):
    terms, advantage = refs[:-1], refs[-1]
    advantage[...] = jnp.sum(sum(term[...] for term in terms) * shares[...], axis=1, keepdims=True)


def whole(shape):
    return pl.BlockSpec(shape, lambda i, places: (0,) * len(shape))


def weight_specs(tile, depth_steps, features):
    def place(i, places):
        return places[i // depth_steps] * depth_steps + i % depth_steps

    return [
        pl.BlockSpec((1, tile, features), lambda i, places: (0, place(i, places), 0)),
        pl.BlockSpec((tile, 2 * HD), lambda i, places: (place(i, places), 0)),
    ]


def estimate(seq, depth, width):
    return pl.CostEstimate(flops=2 * seq * depth * width, bytes_accessed=2 * depth * width, transcendentals=0)


def body(hidden, query_weight, keyval_weight, reward_head, lengths, group_ids, dest):
    sections = lax.axis_size("section")
    dp_size = lax.axis_size("dp")
    mp_size = lax.axis_size("mp")
    section_idx = lax.axis_index("section")
    dp_idx = lax.axis_index("dp")
    mp_idx = lax.axis_index("mp")
    total_rows = lengths.shape[0]
    own = section_idx * dp_size + dp_idx
    other = (1 - section_idx) * dp_size + dp_idx

    seq, depth = hidden.shape[1], hidden.shape[2]
    features = query_weight.shape[2]
    width = features + 2 * HD
    half = seq // 2
    keyval_weight = keyval_weight.reshape(keyval_weight.shape[1], 2 * HD)

    up = functools.partial(lax.ppermute, axis_name="mp", perm=ring(mp_size, 1))
    down = functools.partial(lax.ppermute, axis_name="mp", perm=ring(mp_size, -1))
    across = functools.partial(lax.ppermute, axis_name=PLANE, perm=x_opposite(sections, dp_size))

    block_count = dest.shape[0]
    most = max(2, 2 * block_count // total_rows)
    targets = dest[:, 0]
    order = jnp.arange(block_count, dtype=jnp.int32)
    same = (targets[:, None] == targets[None, :]) & (order[None, :] < order[:, None])
    slot = targets * most + jnp.sum(same.astype(jnp.int32), axis=1)
    held = jnp.where(section_idx == 0, order, (order + block_count // 2) % block_count)
    hit = jnp.arange(total_rows * most, dtype=jnp.int32)[:, None] == slot[None, :]
    source = jnp.sum(jnp.where(hit, held[None, :] + 1, 0), axis=1) - 1

    mine = hidden[0]
    below, above = up(mine), down(mine)
    mine_across, keyval_weight = lax.optimization_barrier((mine, keyval_weight))
    theirs = across(mine_across)

    below_idx, above_idx, far_idx = (mp_idx + mp_size - 1) % mp_size, (mp_idx + 1) % mp_size, (mp_idx + 2) % mp_size
    head = reward_head.reshape(1, features)
    reward_scale = jnp.where(section_idx == 1, 1.0 / lengths.astype(jnp.float32), 0.0)

    rows = jnp.arange(total_rows)
    shares = jnp.where(rows == own, 1.0, 0.0) - jnp.where(group_ids == group_ids[own], 1.0 / GSIZE, 0.0)
    shares = jnp.pad(shares, (0, LANES - total_rows)).reshape(1, LANES)

    def indices(*values):
        return jnp.stack([jnp.asarray(value, jnp.int32) for value in values])

    def call(kernel, tile, pieces, places, operands, in_specs, out_specs, out_shape, scratch=()):
        depth_steps = depth // tile
        return pl.pallas_call(
            functools.partial(kernel, depth_steps),
            grid_spec=pltpu.PrefetchScalarGridSpec(
                num_scalar_prefetch=1,
                grid=(depth_steps * pieces,),
                in_specs=in_specs[:-1] + weight_specs(tile, depth_steps, features) + in_specs[-1],
                out_specs=out_specs,
                scratch_shapes=scratch,
            ),
            out_shape=out_shape,
            compiler_params=pltpu.CompilerParams(vmem_limit_bytes=VMEM_LIMIT),
            cost_estimate=estimate(seq, depth * pieces, width),
        )(places, *operands[:-1], query_weight, keyval_weight, *operands[-1])

    total_spec = whole((seq, width))

    def start(piece):
        return call(
            start_kernel, START_TILE, 1, indices(mp_idx), [piece, []], [whole((seq, depth)), []],
            total_spec, jax.ShapeDtypeStruct((seq, width), jnp.float32),
        )

    def middle(parts, total):
        return call(
            lambda steps, *refs: project_kernel(steps, 2, *refs), MIDDLE_TILE, 2, indices(below_idx, above_idx),
            [*parts, total, []], [whole(part.shape) for part in parts] + [total_spec, []],
            total_spec, jax.ShapeDtypeStruct((seq, width), jnp.float32),
        )

    def finish(parts, partial, row, earlier):
        return call(
            row_kernel, LAST_TILE, 1, indices(far_idx, lengths[row], row),
            [*parts, partial, [head, reward_scale[row].reshape(1, 1), earlier]],
            [whole(part.shape) for part in parts]
            + [total_spec, [whole((1, features)), whole((1, 1)), whole((1, LANES))]],
            [whole((seq, features)), whole((1, LANES))],
            [jax.ShapeDtypeStruct((seq, features), jnp.bfloat16), jax.ShapeDtypeStruct((1, LANES), jnp.float32)],
            [pltpu.VMEM((seq, width), jnp.float32)],
        )

    def ahead(*arrays):
        return lax.optimization_barrier(arrays)

    own_start = start(mine)
    below, above, own_start = ahead(below, above, own_start)
    far_low, far_high = up(below[:half]), down(above[half:])
    crossed = across(jnp.concatenate([below[:END], above[seq - END:]], axis=0))
    own_partial = middle([below, above], own_start)
    their_below_high, their_above_low = up(theirs[END:]), down(theirs[:seq - END])
    far_middle = across(jnp.concatenate([far_low[PASSED:], far_high[:half - PASSED]], axis=0))
    own_states, own_reward = finish([far_low, far_high], own_partial, own, jnp.zeros((1, LANES), jnp.float32))
    their_start = start(theirs)
    crossed, own_states = ahead(crossed, own_states)
    their_far_low, their_far_high = up(crossed[:PASSED]), down(crossed[2 * END - PASSED:])
    their_partial = middle([crossed[:END], their_below_high, their_above_low, crossed[END:]], their_start)
    their_states, rewards = finish([their_far_low, far_middle, their_far_high], their_partial, other, own_reward)

    block_spec = pl.BlockSpec((seq, features), lambda i, slots: (0, 0))
    outgoing = pl.pallas_call(
        place_kernel,
        grid_spec=pltpu.PrefetchScalarGridSpec(
            num_scalar_prefetch=1,
            grid=(1,),
            in_specs=[block_spec, block_spec],
            out_specs=pl.BlockSpec((total_rows, most, BLK, features), lambda i, slots: (0, 0, 0, 0)),
        ),
        out_shape=jax.ShapeDtypeStruct((total_rows, most, BLK, features), jnp.bfloat16),
        compiler_params=pltpu.CompilerParams(vmem_limit_bytes=VMEM_LIMIT),
        cost_estimate=pl.CostEstimate(flops=0, bytes_accessed=6 * seq * features, transcendentals=0),
    )(source, own_states, their_states)
    cores = 2
    across_size = sections * 2
    along = sections * dp_size // (cores * across_size)

    def exchanged(terms, span, size):
        pairs = [turn(sections * dp_size, span, size, step) for step in range(1, size)]
        return [terms] + [lax.ppermute(terms, PLANE, pair) for pair in pairs]

    rewards = sum(exchanged(rewards, cores, along))
    outgoing, rewards = ahead(outgoing, rewards)
    received = lax.all_to_all(outgoing, PLANE, split_axis=0, concat_axis=0, tiled=True)
    rewards += sum(lax.ppermute(rewards, "mp", ring(mp_size, step)) for step in range(1, mp_size))
    rewards = sum(exchanged(rewards, 1, cores))
    terms = exchanged(rewards, cores * along, across_size)
    advantage = pl.pallas_call(
        advantage_kernel, out_shape=jax.ShapeDtypeStruct((1, 1), jnp.float32)
    )(shares, *terms)
    return (received[None], advantage.reshape(1))


def solution(mesh):
    return jax.shard_map(
        body,
        mesh=mesh,
        in_specs=(
            P(("section", "dp"), None, "mp"),
            P("section", None, "mp"),
            P("section", None, None, "mp"),
            P("mp"),
            P(),
            P(),
            P(("section", "dp"), None),
        ),
        out_specs=(P(("section", "dp"), None, None, None, "mp"), P(("section", "dp"))),
        check_vma=False,
    )
```

```python
import functools
import math

import jax
import jax.numpy as jnp
from jax import lax
from jax.experimental import pallas as pl
from jax.experimental.pallas import tpu as pltpu
from jax.sharding import PartitionSpec as P

HD = 128
BLK = 16
GSIZE = 4
LANES = 128
START_TILE = 1024
MIDDLE_TILE = 2048
LAST_TILE = 1024
END = 80
PASSED = 64
PLANE = ("section", "dp")
VMEM_LIMIT = 32 * 1024 * 1024


def x_opposite(sections, dp_size):
    count = sections * dp_size
    return [(i, (i + dp_size) % count) for i in range(count)]


def ring(size, step):
    return [(i, (i + step) % size) for i in range(size)]


def turn(count, span, size, step):
    return [(i, i + ((i // span + step) % size - i // span % size) * span) for i in range(count)]


def project(parts, query_weight, keyval_weight, total):
    features = query_weight.shape[-1]
    rows = jnp.concatenate(parts, axis=0)
    total[:, :features] += jnp.dot(rows, query_weight[0], preferred_element_type=jnp.float32)
    total[:, features:] += jnp.dot(rows, keyval_weight[...], preferred_element_type=jnp.float32)


def project_kernel(depth_steps, number, places, *refs):
    parts, (partial, query_weight, keyval_weight, total) = refs[:-4], refs[-4:]
    step = pl.program_id(0)

    @pl.when(step == 0)
    def _():
        total[...] = jnp.zeros_like(total) if partial is None else partial[...]

    each = len(parts) // number
    depth = query_weight.shape[1]
    columns = pl.ds(pl.multiple_of(lax.rem(step, depth_steps) * depth, depth), depth)
    for piece in range(number):
        @pl.when(step // depth_steps == piece)
        def _():
            held = [part[:, columns] for part in parts[piece * each:(piece + 1) * each]]
            project(held, query_weight, keyval_weight, total)


def start_kernel(depth_steps, places, *refs):
    project_kernel(depth_steps, 1, places, *refs[:-3], None, *refs[-3:])


def attend(total, features, length, states, base):
    seq = total.shape[0]
    half = seq // 2
    keys = total[:, features:features + HD].astype(jnp.bfloat16)
    values = total[:, features + HD:features + 2 * HD].astype(jnp.bfloat16)
    values = jnp.concatenate([values, jnp.ones_like(values)], axis=1)
    scale = math.log2(math.e) / math.sqrt(HD)
    for head in range(features // HD):
        cols = pl.ds(head * HD, HD)
        for begin, size in ((0, half), (half, half)):
            reach = begin + size
            query = total[begin:reach, cols].astype(jnp.bfloat16)
            scores = lax.dot_general(
                query, keys[:reach], (((1,), (1,)), ((), ())), preferred_element_type=jnp.float32
            )
            token = lax.broadcasted_iota(jnp.int32, scores.shape, 0) + begin
            place = lax.broadcasted_iota(jnp.int32, scores.shape, 1)
            scores = jnp.where(place <= token, scores, -1e30)
            highest = jnp.max(scores, axis=1, keepdims=True)
            weights = jnp.exp2((scores - highest) * scale).astype(jnp.bfloat16)
            mixed = jnp.dot(weights, values[:reach], preferred_element_type=jnp.float32)
            output = mixed[:, :HD] / mixed[:, HD:]
            token = lax.broadcasted_iota(jnp.int32, output.shape, 0) + begin
            output = jnp.where(token < length, output, 0.0)
            states[pl.ds(base + begin, size), cols] = output.astype(jnp.bfloat16)


def row_reward(states, base, seq, head, scale, place):
    terms = states[pl.ds(base, seq), :].astype(jnp.float32) * head[...]
    summed = jnp.sum(jnp.sum(terms, axis=0, keepdims=True), axis=1, keepdims=True) * scale
    lane = lax.broadcasted_iota(jnp.int32, (1, LANES), 1)
    return jnp.where(lane == place, jnp.broadcast_to(summed, (1, LANES)), 0.0)


def row_kernel(depth_steps, places, *refs):
    parts, (head, scale, earlier, states, reward, total) = refs[:-6], refs[-6:]
    project_kernel(depth_steps, 1, places, *parts, total)

    @pl.when(pl.program_id(0) == pl.num_programs(0) - 1)
    def _():
        attend(total, states.shape[1], places[1], states, 0)
        reward[...] = earlier[...] + row_reward(states, 0, total.shape[0], head, scale[...], places[2])


def place_kernel(slots, first, second, outgoing):
    shards, most = outgoing.shape[0], outgoing.shape[1]
    seq = first.shape[0]

    def fill(shard, carry):
        for k in range(most):
            block = slots[shard * most + k]
            rows = pl.ds(pl.multiple_of(lax.rem(jnp.maximum(block, 0), seq // BLK) * BLK, BLK), BLK)
            held = jnp.where(block < seq // BLK, first[rows, :], second[rows, :])
            outgoing[shard, k] = jnp.where(block >= 0, held, jnp.zeros_like(held))
        return carry

    lax.fori_loop(0, shards, fill, 0, unroll=4)


def advantage_kernel(shares, *refs):
    terms, advantage = refs[:-1], refs[-1]
    advantage[...] = jnp.sum(sum(term[...] for term in terms) * shares[...], axis=1, keepdims=True)


def whole(shape):
    return pl.BlockSpec(shape, lambda i, places: (0,) * len(shape))


def weight_specs(tile, depth_steps, features):
    def place(i, places):
        return places[i // depth_steps] * depth_steps + i % depth_steps

    return [
        pl.BlockSpec((1, tile, features), lambda i, places: (0, place(i, places), 0)),
        pl.BlockSpec((tile, 2 * HD), lambda i, places: (place(i, places), 0)),
    ]


def estimate(seq, depth, width):
    return pl.CostEstimate(flops=2 * seq * depth * width, bytes_accessed=2 * depth * width, transcendentals=0)


def body(hidden, query_weight, keyval_weight, reward_head, lengths, group_ids, dest):
    sections = lax.axis_size("section")
    dp_size = lax.axis_size("dp")
    mp_size = lax.axis_size("mp")
    section_idx = lax.axis_index("section")
    dp_idx = lax.axis_index("dp")
    mp_idx = lax.axis_index("mp")
    total_rows = lengths.shape[0]
    own = section_idx * dp_size + dp_idx
    other = (1 - section_idx) * dp_size + dp_idx

    seq, depth = hidden.shape[1], hidden.shape[2]
    features = query_weight.shape[2]
    width = features + 2 * HD
    half = seq // 2
    keyval_weight = keyval_weight.reshape(keyval_weight.shape[1], 2 * HD)

    up = functools.partial(lax.ppermute, axis_name="mp", perm=ring(mp_size, 1))
    down = functools.partial(lax.ppermute, axis_name="mp", perm=ring(mp_size, -1))
    across = functools.partial(lax.ppermute, axis_name=PLANE, perm=x_opposite(sections, dp_size))

    block_count = dest.shape[0]
    most = max(2, 2 * block_count // total_rows)
    targets = dest[:, 0]
    order = jnp.arange(block_count, dtype=jnp.int32)
    same = (targets[:, None] == targets[None, :]) & (order[None, :] < order[:, None])
    slot = targets * most + jnp.sum(same.astype(jnp.int32), axis=1)
    held = jnp.where(section_idx == 0, order, (order + block_count // 2) % block_count)
    hit = jnp.arange(total_rows * most, dtype=jnp.int32)[:, None] == slot[None, :]
    source = jnp.sum(jnp.where(hit, held[None, :] + 1, 0), axis=1) - 1

    mine = hidden[0]
    below, above = up(mine), down(mine)
    mine_across, keyval_weight = lax.optimization_barrier((mine, keyval_weight))
    theirs = across(mine_across)

    below_idx, above_idx, far_idx = (mp_idx + mp_size - 1) % mp_size, (mp_idx + 1) % mp_size, (mp_idx + 2) % mp_size
    head = reward_head.reshape(1, features)
    reward_scale = jnp.where(section_idx == 1, 1.0 / lengths.astype(jnp.float32), 0.0)

    rows = jnp.arange(total_rows)
    shares = jnp.where(rows == own, 1.0, 0.0) - jnp.where(group_ids == group_ids[own], 1.0 / GSIZE, 0.0)
    shares = jnp.pad(shares, (0, LANES - total_rows)).reshape(1, LANES)

    def indices(*values):
        return jnp.stack([jnp.asarray(value, jnp.int32) for value in values])

    def call(kernel, tile, pieces, places, operands, in_specs, out_specs, out_shape, scratch=()):
        depth_steps = depth // tile
        return pl.pallas_call(
            functools.partial(kernel, depth_steps),
            grid_spec=pltpu.PrefetchScalarGridSpec(
                num_scalar_prefetch=1,
                grid=(depth_steps * pieces,),
                in_specs=in_specs[:-1] + weight_specs(tile, depth_steps, features) + in_specs[-1],
                out_specs=out_specs,
                scratch_shapes=scratch,
            ),
            out_shape=out_shape,
            compiler_params=pltpu.CompilerParams(vmem_limit_bytes=VMEM_LIMIT),
            cost_estimate=estimate(seq, depth * pieces, width),
        )(places, *operands[:-1], query_weight, keyval_weight, *operands[-1])

    total_spec = whole((seq, width))

    def start(piece):
        return call(
            start_kernel, START_TILE, 1, indices(mp_idx), [piece, []], [whole((seq, depth)), []],
            total_spec, jax.ShapeDtypeStruct((seq, width), jnp.float32),
        )

    def middle(parts, total):
        return call(
            lambda steps, *refs: project_kernel(steps, 2, *refs), MIDDLE_TILE, 2, indices(below_idx, above_idx),
            [*parts, total, []], [whole(part.shape) for part in parts] + [total_spec, []],
            total_spec, jax.ShapeDtypeStruct((seq, width), jnp.float32),
        )

    def finish(parts, partial, row, earlier):
        return call(
            row_kernel, LAST_TILE, 1, indices(far_idx, lengths[row], row),
            [*parts, partial, [head, reward_scale[row].reshape(1, 1), earlier]],
            [whole(part.shape) for part in parts]
            + [total_spec, [whole((1, features)), whole((1, 1)), whole((1, LANES))]],
            [whole((seq, features)), whole((1, LANES))],
            [jax.ShapeDtypeStruct((seq, features), jnp.bfloat16), jax.ShapeDtypeStruct((1, LANES), jnp.float32)],
            [pltpu.VMEM((seq, width), jnp.float32)],
        )

    def ahead(*arrays):
        return lax.optimization_barrier(arrays)

    own_start = start(mine)
    below, above, own_start = ahead(below, above, own_start)
    far_low, far_high = up(below[:half]), down(above[half:])
    crossed = across(jnp.concatenate([below[:END], above[seq - END:]], axis=0))
    own_partial = middle([below, above], own_start)
    their_below_high, their_above_low = up(theirs[END:]), down(theirs[:seq - END])
    far_middle = across(jnp.concatenate([far_low[PASSED:], far_high[:half - PASSED]], axis=0))
    their_start = start(theirs)
    crossed, own_partial = ahead(crossed, own_partial)
    their_far_low, their_far_high = up(crossed[:PASSED]), down(crossed[2 * END - PASSED:])
    own_states, own_reward = finish([far_low, far_high], own_partial, own, jnp.zeros((1, LANES), jnp.float32))
    their_partial = middle([crossed[:END], their_below_high, their_above_low, crossed[END:]], their_start)
    their_states, rewards = finish([their_far_low, far_middle, their_far_high], their_partial, other, own_reward)

    block_spec = pl.BlockSpec((seq, features), lambda i, slots: (0, 0))
    outgoing = pl.pallas_call(
        place_kernel,
        grid_spec=pltpu.PrefetchScalarGridSpec(
            num_scalar_prefetch=1,
            grid=(1,),
            in_specs=[block_spec, block_spec],
            out_specs=pl.BlockSpec((total_rows, most, BLK, features), lambda i, slots: (0, 0, 0, 0)),
        ),
        out_shape=jax.ShapeDtypeStruct((total_rows, most, BLK, features), jnp.bfloat16),
        compiler_params=pltpu.CompilerParams(vmem_limit_bytes=VMEM_LIMIT),
        cost_estimate=pl.CostEstimate(flops=0, bytes_accessed=6 * seq * features, transcendentals=0),
    )(source, own_states, their_states)
    cores = 2
    across_size = sections * 2
    along = sections * dp_size // (cores * across_size)

    def exchanged(terms, span, size):
        pairs = [turn(sections * dp_size, span, size, step) for step in range(1, size)]
        return [terms] + [lax.ppermute(terms, PLANE, pair) for pair in pairs]

    rewards = sum(exchanged(rewards, cores, along))
    outgoing, rewards = ahead(outgoing, rewards)
    received = lax.all_to_all(outgoing, PLANE, split_axis=0, concat_axis=0, tiled=True)
    rewards += sum(lax.ppermute(rewards, "mp", ring(mp_size, step)) for step in range(1, mp_size))
    rewards = sum(exchanged(rewards, 1, cores))
    terms = exchanged(rewards, cores * along, across_size)
    advantage = pl.pallas_call(
        advantage_kernel, out_shape=jax.ShapeDtypeStruct((1, 1), jnp.float32)
    )(shares, *terms)
    return (received[None], advantage.reshape(1))


def solution(mesh):
    return jax.shard_map(
        body,
        mesh=mesh,
        in_specs=(
            P(("section", "dp"), None, "mp"),
            P("section", None, "mp"),
            P("section", None, None, "mp"),
            P("mp"),
            P(),
            P(),
            P(("section", "dp"), None),
        ),
        out_specs=(P(("section", "dp"), None, None, None, "mp"), P(("section", "dp"))),
        check_vma=False,
    )
```

```python
import functools
import math

import jax
import jax.numpy as jnp
from jax import lax
from jax.experimental import pallas as pl
from jax.experimental.pallas import tpu as pltpu
from jax.sharding import PartitionSpec as P

HD = 128
BLK = 16
GSIZE = 4
LANES = 128
START_TILE = 1024
MIDDLE_TILE = 2048
LAST_TILE = 1024
END = 80
PASSED = 64
PLANE = ("section", "dp")
VMEM_LIMIT = 40 * 1024 * 1024


def x_opposite(sections, dp_size):
    count = sections * dp_size
    return [(i, (i + dp_size) % count) for i in range(count)]


def ring(size, step):
    return [(i, (i + step) % size) for i in range(size)]


def turn(count, span, size, step):
    return [(i, i + ((i // span + step) % size - i // span % size) * span) for i in range(count)]


def project(parts, query_weight, keyval_weight, total):
    features = query_weight.shape[-1]
    rows = jnp.concatenate(parts, axis=0)
    total[:, :features] += jnp.dot(rows, query_weight[0], preferred_element_type=jnp.float32)
    total[:, features:] += jnp.dot(rows, keyval_weight[...], preferred_element_type=jnp.float32)


def project_kernel(depth_steps, number, places, *refs):
    parts, (partial, query_weight, keyval_weight, total) = refs[:-4], refs[-4:]
    step = pl.program_id(0)

    @pl.when(step == 0)
    def _():
        total[...] = jnp.zeros_like(total) if partial is None else partial[...]

    each = len(parts) // number
    depth = query_weight.shape[1]
    columns = pl.ds(pl.multiple_of(lax.rem(step, depth_steps) * depth, depth), depth)
    for piece in range(number):
        @pl.when(step // depth_steps == piece)
        def _():
            held = [part[:, columns] for part in parts[piece * each:(piece + 1) * each]]
            project(held, query_weight, keyval_weight, total)


def start_kernel(depth_steps, places, *refs):
    project_kernel(depth_steps, 1, places, *refs[:-3], None, *refs[-3:])


def attend(total, features, length, states, base):
    seq = total.shape[0]
    half = seq // 2
    keys = total[:, features:features + HD].astype(jnp.bfloat16)
    values = total[:, features + HD:features + 2 * HD].astype(jnp.bfloat16)
    values = jnp.concatenate([values, jnp.ones_like(values)], axis=1)
    scale = math.log2(math.e) / math.sqrt(HD)
    for head in range(features // HD):
        cols = pl.ds(head * HD, HD)
        for begin, size in ((0, half), (half, half)):
            reach = begin + size
            query = total[begin:reach, cols].astype(jnp.bfloat16)
            scores = lax.dot_general(
                query, keys[:reach], (((1,), (1,)), ((), ())), preferred_element_type=jnp.float32
            )
            token = lax.broadcasted_iota(jnp.int32, scores.shape, 0) + begin
            place = lax.broadcasted_iota(jnp.int32, scores.shape, 1)
            scores = jnp.where(place <= token, scores, -1e30)
            highest = jnp.max(scores, axis=1, keepdims=True)
            weights = jnp.exp2((scores - highest) * scale).astype(jnp.bfloat16)
            mixed = jnp.dot(weights, values[:reach], preferred_element_type=jnp.float32)
            output = mixed[:, :HD] / mixed[:, HD:]
            token = lax.broadcasted_iota(jnp.int32, output.shape, 0) + begin
            output = jnp.where(token < length, output, 0.0)
            states[pl.ds(base + begin, size), cols] = output.astype(jnp.bfloat16)


def row_reward(states, base, seq, head, scale, place):
    terms = states[pl.ds(base, seq), :].astype(jnp.float32) * head[...]
    summed = jnp.sum(jnp.sum(terms, axis=0, keepdims=True), axis=1, keepdims=True) * scale
    lane = lax.broadcasted_iota(jnp.int32, (1, LANES), 1)
    return jnp.where(lane == place, jnp.broadcast_to(summed, (1, LANES)), 0.0)


def row_kernel(depth_steps, places, *refs):
    parts, (head, scale, earlier, states, reward, total) = refs[:-6], refs[-6:]
    project_kernel(depth_steps, 1, places, *parts, total)

    @pl.when(pl.program_id(0) == pl.num_programs(0) - 1)
    def _():
        attend(total, states.shape[1], places[1], states, 0)
        reward[...] = earlier[...] + row_reward(states, 0, total.shape[0], head, scale[...], places[2])


def place_kernel(slots, first, second, outgoing):
    shards, most = outgoing.shape[0], outgoing.shape[1]
    seq = first.shape[0]

    def fill(shard, carry):
        for k in range(most):
            block = slots[shard * most + k]
            rows = pl.ds(pl.multiple_of(lax.rem(jnp.maximum(block, 0), seq // BLK) * BLK, BLK), BLK)
            held = jnp.where(block < seq // BLK, first[rows, :], second[rows, :])
            outgoing[shard, k] = jnp.where(block >= 0, held, jnp.zeros_like(held))
        return carry

    lax.fori_loop(0, shards, fill, 0, unroll=4)


def advantage_kernel(shares, *refs):
    terms, advantage = refs[:-1], refs[-1]
    advantage[...] = jnp.sum(sum(term[...] for term in terms) * shares[...], axis=1, keepdims=True)


def whole(shape):
    return pl.BlockSpec(shape, lambda i, places: (0,) * len(shape))


def weight_specs(tile, depth_steps, features):
    def place(i, places):
        return places[i // depth_steps] * depth_steps + i % depth_steps

    return [
        pl.BlockSpec((1, tile, features), lambda i, places: (0, place(i, places), 0)),
        pl.BlockSpec((tile, 2 * HD), lambda i, places: (place(i, places), 0)),
    ]


def estimate(seq, depth, width):
    return pl.CostEstimate(flops=2 * seq * depth * width, bytes_accessed=2 * depth * width, transcendentals=0)


def body(hidden, query_weight, keyval_weight, reward_head, lengths, group_ids, dest):
    sections = lax.axis_size("section")
    dp_size = lax.axis_size("dp")
    mp_size = lax.axis_size("mp")
    section_idx = lax.axis_index("section")
    dp_idx = lax.axis_index("dp")
    mp_idx = lax.axis_index("mp")
    total_rows = lengths.shape[0]
    own = section_idx * dp_size + dp_idx
    other = (1 - section_idx) * dp_size + dp_idx

    seq, depth = hidden.shape[1], hidden.shape[2]
    features = query_weight.shape[2]
    width = features + 2 * HD
    half = seq // 2
    keyval_weight = keyval_weight.reshape(keyval_weight.shape[1], 2 * HD)

    up = functools.partial(lax.ppermute, axis_name="mp", perm=ring(mp_size, 1))
    down = functools.partial(lax.ppermute, axis_name="mp", perm=ring(mp_size, -1))
    across = functools.partial(lax.ppermute, axis_name=PLANE, perm=x_opposite(sections, dp_size))

    block_count = dest.shape[0]
    most = max(2, 2 * block_count // total_rows)
    targets = dest[:, 0]
    order = jnp.arange(block_count, dtype=jnp.int32)
    same = (targets[:, None] == targets[None, :]) & (order[None, :] < order[:, None])
    slot = targets * most + jnp.sum(same.astype(jnp.int32), axis=1)
    held = jnp.where(section_idx == 0, order, (order + block_count // 2) % block_count)
    hit = jnp.arange(total_rows * most, dtype=jnp.int32)[:, None] == slot[None, :]
    source = jnp.sum(jnp.where(hit, held[None, :] + 1, 0), axis=1) - 1

    mine = hidden[0]
    below, above = up(mine), down(mine)
    mine_across, keyval_weight = lax.optimization_barrier((mine, keyval_weight))
    theirs = across(mine_across)

    below_idx, above_idx, far_idx = (mp_idx + mp_size - 1) % mp_size, (mp_idx + 1) % mp_size, (mp_idx + 2) % mp_size
    head = reward_head.reshape(1, features)
    reward_scale = jnp.where(section_idx == 1, 1.0 / lengths.astype(jnp.float32), 0.0)

    rows = jnp.arange(total_rows)
    shares = jnp.where(rows == own, 1.0, 0.0) - jnp.where(group_ids == group_ids[own], 1.0 / GSIZE, 0.0)
    shares = jnp.pad(shares, (0, LANES - total_rows)).reshape(1, LANES)

    def indices(*values):
        return jnp.stack([jnp.asarray(value, jnp.int32) for value in values])

    def call(kernel, tile, pieces, places, operands, in_specs, out_specs, out_shape, scratch=()):
        depth_steps = depth // tile
        return pl.pallas_call(
            functools.partial(kernel, depth_steps),
            grid_spec=pltpu.PrefetchScalarGridSpec(
                num_scalar_prefetch=1,
                grid=(depth_steps * pieces,),
                in_specs=in_specs[:-1] + weight_specs(tile, depth_steps, features) + in_specs[-1],
                out_specs=out_specs,
                scratch_shapes=scratch,
            ),
            out_shape=out_shape,
            compiler_params=pltpu.CompilerParams(vmem_limit_bytes=VMEM_LIMIT),
            cost_estimate=estimate(seq, depth * pieces, width),
        )(places, *operands[:-1], query_weight, keyval_weight, *operands[-1])

    total_spec = whole((seq, width))

    def start(piece):
        return call(
            start_kernel, START_TILE, 1, indices(mp_idx), [piece, []], [whole((seq, depth)), []],
            total_spec, jax.ShapeDtypeStruct((seq, width), jnp.float32),
        )

    def middle(parts, total):
        return call(
            lambda steps, *refs: project_kernel(steps, 2, *refs), MIDDLE_TILE, 2, indices(below_idx, above_idx),
            [*parts, total, []], [whole(part.shape) for part in parts] + [total_spec, []],
            total_spec, jax.ShapeDtypeStruct((seq, width), jnp.float32),
        )

    def finish(parts, partial, row, earlier):
        return call(
            row_kernel, LAST_TILE, 1, indices(far_idx, lengths[row], row),
            [*parts, partial, [head, reward_scale[row].reshape(1, 1), earlier]],
            [whole(part.shape) for part in parts]
            + [total_spec, [whole((1, features)), whole((1, 1)), whole((1, LANES))]],
            [whole((seq, features)), whole((1, LANES))],
            [jax.ShapeDtypeStruct((seq, features), jnp.bfloat16), jax.ShapeDtypeStruct((1, LANES), jnp.float32)],
            [pltpu.VMEM((seq, width), jnp.float32)],
        )

    def ahead(*arrays):
        return lax.optimization_barrier(arrays)

    own_start = start(mine)
    below, above, own_start = ahead(below, above, own_start)
    far_low, far_high = up(below[:half]), down(above[half:])
    crossed = across(jnp.concatenate([below[:END], above[seq - END:]], axis=0))
    own_partial = middle([below, above], own_start)
    their_below_high, their_above_low = up(theirs[END:]), down(theirs[:seq - END])
    far_middle = across(jnp.concatenate([far_low[PASSED:], far_high[:half - PASSED]], axis=0))
    their_start = start(theirs)
    crossed, own_partial = ahead(crossed, own_partial)
    their_far_low, their_far_high = up(crossed[:PASSED]), down(crossed[2 * END - PASSED:])
    own_states, own_reward = finish([far_low, far_high], own_partial, own, jnp.zeros((1, LANES), jnp.float32))
    their_partial = middle([crossed[:END], their_below_high, their_above_low, crossed[END:]], their_start)
    their_states, rewards = finish([their_far_low, far_middle, their_far_high], their_partial, other, own_reward)

    block_spec = pl.BlockSpec((seq, features), lambda i, slots: (0, 0))
    outgoing = pl.pallas_call(
        place_kernel,
        grid_spec=pltpu.PrefetchScalarGridSpec(
            num_scalar_prefetch=1,
            grid=(1,),
            in_specs=[block_spec, block_spec],
            out_specs=pl.BlockSpec((total_rows, most, BLK, features), lambda i, slots: (0, 0, 0, 0)),
        ),
        out_shape=jax.ShapeDtypeStruct((total_rows, most, BLK, features), jnp.bfloat16),
        compiler_params=pltpu.CompilerParams(vmem_limit_bytes=VMEM_LIMIT),
        cost_estimate=pl.CostEstimate(flops=0, bytes_accessed=6 * seq * features, transcendentals=0),
    )(source, own_states, their_states)
    cores = 2
    across_size = sections * 2
    along = sections * dp_size // (cores * across_size)

    def exchanged(terms, span, size):
        pairs = [turn(sections * dp_size, span, size, step) for step in range(1, size)]
        return [terms] + [lax.ppermute(terms, PLANE, pair) for pair in pairs]

    rewards = sum(exchanged(rewards, cores, along))
    outgoing, rewards = ahead(outgoing, rewards)
    received = lax.all_to_all(outgoing, PLANE, split_axis=0, concat_axis=0, tiled=True)
    rewards += sum(lax.ppermute(rewards, "mp", ring(mp_size, step)) for step in range(1, mp_size))
    rewards = sum(exchanged(rewards, 1, cores))
    terms = exchanged(rewards, cores * along, across_size)
    advantage = pl.pallas_call(
        advantage_kernel, out_shape=jax.ShapeDtypeStruct((1, 1), jnp.float32)
    )(shares, *terms)
    return (received[None], advantage.reshape(1))


def solution(mesh):
    return jax.shard_map(
        body,
        mesh=mesh,
        in_specs=(
            P(("section", "dp"), None, "mp"),
            P("section", None, "mp"),
            P("section", None, None, "mp"),
            P("mp"),
            P(),
            P(),
            P(("section", "dp"), None),
        ),
        out_specs=(P(("section", "dp"), None, None, None, "mp"), P(("section", "dp"))),
        check_vma=False,
    )
```
